512 devices in a mesh: wide: 32 (over y_hi, x, core), narrow: 16 (over z, y_lo).
Axes of the slice: x: 4, y: 8 (y_hi: 4, y_lo: 2; y = y_hi * 2 + y_lo), z: 8, core: 2. Of those that a mesh axis runs over, the one named last changes fastest.
Arguments:
- layer_input: bfloat16 [1536, 10240], P('wide', 'narrow'), may hold values from -3 to 3
- output_grad: bfloat16 [1536, 10240], P('wide', 'narrow'), may hold values from -0.75 to 0.75
- pre_activation: bfloat16 [1536, 20480], P('narrow', 'wide'), may hold values from -6 to 6
- w_up: bfloat16 [10240, 20480], P('narrow', 'wide'), may hold values from -0.15625 to 0.15625
- w_down: bfloat16 [20480, 10240], P('wide', 'narrow'), may hold values from -0.25 to 0.25
Outputs:
- input_grad: bfloat16 [1536, 10240], P('wide', 'narrow')
- up_grad: float32 [10240, 20480], P('narrow', 'wide')
- down_grad: float32 [20480, 10240], P('wide', 'narrow')
The draws below stay inside these ranges and needn't reach their ends.
All inputs are finite; a program needn't handle non-finite values.
Results may differ from the reference program's by a relative error of at most 0.03.
Values may be sent and summed in bfloat16 or wider, within the bound.
No kernel may reach another device: no remote copies, remote signals or barrier semaphores. Data moves between devices by JAX's collectives and lax.ppermute only.
A program may use at most 64 MiB of HBM per device.

```python
import math
import jax
import jax.numpy as jnp
from jax import lax

D = 10240
FF = 20480
TOKENS = 1536
N_WIDE = 32
N_NARROW = 16


def block_levels(rng, extent, split, low, high):
    factor_of = 1.0
    for dim, blocks in split:
        draws = jax.random.uniform(jax.random.fold_in(jax.random.fold_in(rng, 6), dim), (blocks,), jnp.float32, low / len(split), high / len(split))
        factor_of = factor_of * jnp.repeat(jnp.exp(draws), extent[dim] // blocks).reshape((-1,) + (1,) * (len(extent) - 1 - dim))
    return factor_of


def gaussian(key, dims, spread, limit, shards=(), dtype=jnp.bfloat16):
    values = spread * jax.random.normal(key, dims, jnp.float32)
    if shards:
        values = values * block_levels(key, dims, shards, -0.22, 0.18)
    return jnp.clip(values, -limit, limit).astype(dtype)


def setup_inputs(seed: int = 0) -> dict:
    seeds = jax.random.split(jax.random.key(seed), 6)
    layer_input = gaussian(seeds[0], (TOKENS, D), 0.2, 3.0, ((0, 32), (1, 16)))
    output_grad = gaussian(seeds[1], (TOKENS, D), 0.05, 0.75, ((0, 32), (1, 16)))
    pre_activation = gaussian(seeds[2], (TOKENS, FF), 1.0, 6.0, ((0, 16), (1, 32)))
    w_up = gaussian(seeds[3], (D, FF), (FF // 16) ** -0.5, 0.15625, ((0, 16), (1, 32)))
    w_down = gaussian(seeds[4], (FF, D), (D // 16) ** -0.5, 0.25, ((0, 32), (1, 16)))
    return dict(layer_input=layer_input, output_grad=output_grad, pre_activation=pre_activation, w_up=w_up, w_down=w_down)


def gelu_parts(pre_values):
    values = pre_values.astype(jnp.float32)
    normal_cdf = 0.5 * (1.0 + jax.scipy.special.erf(values / math.sqrt(2.0)))
    normal_pdf = jnp.exp(-0.5 * values * values) / math.sqrt(2.0 * math.pi)
    return (values * normal_cdf, normal_cdf + values * normal_pdf)

def blocked_product(left, right, blocks):
    block_width = left.shape[1] // blocks
    total = jnp.zeros((left.shape[0], right.shape[0]), jnp.float32)
    for block_index in range(blocks):
        first = block_index * block_width
        part_sum = jnp.dot(left[:, first:first + block_width], right[:, first:first + block_width].T, preferred_element_type=jnp.float32)
        total = total + lax.optimization_barrier(part_sum.astype(jnp.bfloat16)).astype(jnp.float32)
    return total

def reference(layer_input, output_grad, pre_activation, w_up, w_down):
    gelu_value, gelu_slope = gelu_parts(pre_activation)
    act_values = gelu_value.astype(jnp.bfloat16)
    act_grad = blocked_product(output_grad, w_down, N_NARROW)
    slope_grad = (act_grad * gelu_slope).astype(jnp.bfloat16)
    down_grad = jnp.dot(act_values.T, output_grad, preferred_element_type=jnp.float32)
    up_grad = jnp.dot(layer_input.T, slope_grad, preferred_element_type=jnp.float32)
    input_grad = blocked_product(slope_grad, w_up, N_WIDE).astype(jnp.bfloat16)
    return (input_grad, up_grad, down_grad)
```

```python
import math

import jax
import jax.numpy as jnp
from jax import lax
from jax.sharding import Mesh, PartitionSpec as P

WIDE = ("yh", "x", "c")
NARROW = ("z", "yl")
CHIPS = ("yh", "x")


def gelu_parts(pre_values):
    values = pre_values.astype(jnp.float32)
    normal_cdf = 0.5 * (1.0 + jax.scipy.special.erf(values / math.sqrt(2.0)))
    normal_pdf = jnp.exp(-0.5 * values * values) / math.sqrt(2.0 * math.pi)
    return (values * normal_cdf, normal_cdf + values * normal_pdf)


def times_transposed(left, right):
    return lax.dot_general(
        left, right, (((1,), (1,)), ((), ())), preferred_element_type=jnp.float32
    )


def over_tokens(left, right):
    dims = tuple(range(left.ndim - 1))
    return lax.dot_general(
        left, right, ((dims, dims), ((), ())), preferred_element_type=jnp.float32
    )


def swap(values, axis):
    return lax.ppermute(values, axis, [(0, 1), (1, 0)])


def scattered(values, axis):
    blocks = lax.all_to_all(values, axis, 0, 0)
    return jnp.sum(blocks.astype(jnp.float32), axis=0)


def per_device(layer_input, output_grad, pre_activation, w_up, w_down):
    core = lax.axis_index("c")
    rows, width = layer_input.shape
    w_down_pair = swap(w_down, "c")
    grad_own = lax.all_to_all(
        jnp.broadcast_to(output_grad, (16, rows, width)), CHIPS, 0, 0
    )
    low, high = pre_activation[:rows], pre_activation[rows:]
    pre_own = jnp.where(core == 0, low, high)
    pre_pair = swap(jnp.where(core == 0, high, low), "c")
    _, slope_own_f = gelu_parts(pre_own)
    _, slope_pair_f = gelu_parts(pre_pair)
    act_tile = gelu_parts(pre_activation)[0].astype(jnp.bfloat16)
    act_all = lax.all_gather(act_tile, NARROW, axis=0, tiled=True)
    input_all = lax.all_gather(layer_input, ("c",) + CHIPS, axis=0, tiled=True)
    w_up_pair = swap(w_up, "c")

    grad_rows = grad_own.reshape(16 * rows, width)
    part_own = times_transposed(grad_rows, w_down).astype(jnp.bfloat16)
    part_pair = times_transposed(grad_rows, w_down_pair).astype(jnp.bfloat16)
    act_grad_own = scattered(part_own.reshape(16, rows, -1), NARROW)
    act_grad_pair = scattered(part_pair.reshape(16, rows, -1), NARROW)
    slope_own = (act_grad_own * slope_own_f).astype(jnp.bfloat16)
    slope_pair = (act_grad_pair * slope_pair_f).astype(jnp.bfloat16)

    def gathered(tile):
        both = lax.all_gather(tile, "yl", axis=0, tiled=True)
        return lax.all_gather(both, "z", axis=0, tiled=True)

    slopes_own = gathered(slope_own)
    slopes_pair = gathered(slope_pair)
    slopes_other = swap(slopes_pair, "c")
    grad_other = swap(grad_rows, "c")

    part_in = times_transposed(slopes_own, w_up) + times_transposed(
        slopes_pair, w_up_pair
    )
    input_grad = scattered(
        part_in.astype(jnp.bfloat16).reshape(16, rows, width), CHIPS
    ).astype(jnp.bfloat16)

    act_parts = act_all.reshape(16, 2, rows, -1)
    grad_parts = [
        jnp.where(core == 0, grad_rows, grad_other),
        jnp.where(core == 0, grad_other, grad_rows),
    ]
    down_grad = sum(
        over_tokens(act_parts[:, i], grad_parts[i].reshape(16, rows, width))
        for i in range(2)
    )
    slope_parts = [
        jnp.where(core == 0, slopes_own, slopes_other),
        jnp.where(core == 0, slopes_other, slopes_own),
    ]
    half = 16 * rows
    up_grad = over_tokens(input_all[:half], slope_parts[0]) + over_tokens(
        input_all[half:], slope_parts[1]
    )
    return (input_grad, up_grad, down_grad)


def solution(mesh):
    fine = Mesh(mesh.devices.reshape(4, 4, 2, 8, 2), WIDE + NARROW)
    tokens = P(WIDE, NARROW)
    hidden = P(NARROW, WIDE)
    return jax.shard_map(
        per_device,
        mesh=fine,
        in_specs=(tokens, tokens, hidden, hidden, tokens),
        out_specs=(tokens, hidden, tokens),
        check_vma=False,
    )
```

```python
import math

import jax
import jax.numpy as jnp
from jax import lax
from jax.sharding import Mesh, PartitionSpec as P

WIDE = ("yh", "x", "c")
NARROW = ("z", "yl")
BF16 = jnp.bfloat16
F32 = jnp.float32


def gelu_parts(pre_values):
    values = pre_values.astype(F32)
    normal_cdf = 0.5 * (1.0 + jax.scipy.special.erf(values / math.sqrt(2.0)))
    normal_pdf = jnp.exp(-0.5 * values * values) / math.sqrt(2.0 * math.pi)
    return (values * normal_cdf, normal_cdf + values * normal_pdf)


def times_transposed(left, right):
    return lax.dot_general(
        left, right, (((1,), (1,)), ((), ())), preferred_element_type=F32
    )


def over_tokens(left, right):
    return lax.dot_general(
        left, right, (((0,), (0,)), ((), ())), preferred_element_type=F32
    )


def swap(values, axis):
    return lax.ppermute(values, axis, [(0, 1), (1, 0)])


def in_order(index, own, other):
    return (jnp.where(index == 0, own, other), jnp.where(index == 0, other, own))


def per_device(layer_input, output_grad, pre_activation, w_up, w_down):
    core, lane = lax.axis_index("c"), lax.axis_index("yl")
    rows, width = layer_input.shape
    half = rows // 2
    hidden = pre_activation.shape[1]

    down_lane = swap(w_down, "yl")
    down_core = swap(w_down, "c")
    pre_lane = swap(pre_activation, "yl")

    pieces = jnp.broadcast_to(output_grad.reshape(2, half, width), (4, 2, half, width))
    grad_y = lax.all_to_all(pieces.reshape(8, half, width), ("yh", "yl"), 0, 0)
    grad_xy = lax.all_to_all(
        jnp.broadcast_to(grad_y, (4, 8, half, width)), "x", 0, 0
    ).reshape(4, 4, 2, half, width)
    grad_xy = jnp.swapaxes(grad_xy, 0, 1)
    grad_own, grad_pair = in_order(lane, grad_xy[:, :, 0], grad_xy[:, :, 1])
    down_both = swap(down_lane, "c")

    pre_both = jnp.stack(in_order(lane, pre_activation, pre_lane))
    pre_cut = pre_both.reshape(2, 2, 2, half, hidden)
    pre_half = jnp.where(lane == 0, pre_cut[:, :, 0], pre_cut[:, :, 1])
    pre_own = jnp.where(core == 0, pre_half[:, 0], pre_half[:, 1])
    pre_sent = jnp.where(core == 0, pre_half[:, 1], pre_half[:, 0])
    pre_pair = swap(pre_sent, "c")
    pre_tile = jnp.concatenate([pre_own, pre_pair], axis=-1).reshape(rows, 2 * hidden)
    slope_factor = gelu_parts(pre_tile)[1]
    act_tile = gelu_parts(pre_both)[0].astype(BF16).reshape(-1, hidden)
    act_all = lax.all_gather(act_tile, "z", axis=0, tiled=True)
    input_all = lax.all_gather(layer_input, WIDE, axis=0, tiled=True)

    up_lane = swap(w_up, "yl")
    up_core = swap(w_up, "c")

    grad_rows = jnp.concatenate([grad_own, grad_pair], axis=-1).reshape(-1, 2 * width)
    down_cat = jnp.concatenate(
        [
            jnp.concatenate([w_down, down_lane], axis=1),
            jnp.concatenate([down_core, down_both], axis=1),
        ],
        axis=0,
    )
    part = times_transposed(grad_rows, down_cat).astype(BF16)
    blocks = lax.all_to_all(part.reshape(8, rows, 2 * hidden), "z", 0, 0)
    act_grad = jnp.sum(blocks.astype(F32), axis=0)
    slope_tile = (act_grad * slope_factor).astype(BF16)
    slopes = lax.all_gather(slope_tile, "z", axis=0, tiled=True)
    up_both = swap(up_lane, "c")
    up_cat = jnp.concatenate(
        [
            jnp.concatenate([w_up, up_core], axis=1),
            jnp.concatenate([up_lane, up_both], axis=1),
        ],
        axis=0,
    )

    grad_lane = swap(grad_pair, "yl")
    shards = grad_own.shape[0] * grad_own.shape[1]
    grad_core = jnp.stack(in_order(lane, grad_own, grad_lane), axis=2)
    grad_other = swap(grad_core, "c")
    grad_all = jnp.stack(in_order(core, grad_core, grad_other), axis=2)
    down_grad = over_tokens(act_all, grad_all.reshape(-1, width))

    part_in = times_transposed(slopes, up_cat).astype(BF16)
    part_in = jnp.swapaxes(part_in.reshape(4, 4, half, 2 * width), 0, 1)
    blocks = lax.all_to_all(part_in, "x", 0, 0)
    part_y = jnp.sum(blocks.astype(F32), axis=0).astype(BF16)
    part_y = jnp.stack(
        in_order(lane, part_y[..., :width], part_y[..., width:]), axis=1
    )
    blocks = lax.all_to_all(part_y.reshape(8, half, width), ("yh", "yl"), 0, 0)
    input_grad = (
        jnp.sum(blocks.reshape(4, rows, width).astype(F32), axis=0)
    ).astype(BF16)

    slopes_lane = swap(slopes, "yl")
    by_shard = [
        jnp.stack(
            in_order(
                lane,
                slopes[:, cut].reshape(shards, half, hidden),
                slopes_lane[:, cut].reshape(shards, half, hidden),
            ),
            axis=1,
        )
        for cut in (slice(0, hidden), slice(hidden, 2 * hidden))
    ]
    slopes_other = swap(by_shard[1], "c")
    slopes_all = jnp.stack(in_order(core, by_shard[0], slopes_other), axis=1)
    up_grad = over_tokens(input_all, slopes_all.reshape(-1, hidden))
    return (input_grad, up_grad, down_grad)


def solution(mesh):
    fine = Mesh(mesh.devices.reshape(4, 4, 2, 8, 2), WIDE + NARROW)
    tokens = P(WIDE, NARROW)
    hidden = P(NARROW, WIDE)
    return jax.shard_map(
        per_device,
        mesh=fine,
        in_specs=(tokens, tokens, hidden, hidden, tokens),
        out_specs=(tokens, hidden, tokens),
        check_vma=False,
    )
```

```python
import math

import jax
import jax.numpy as jnp
from jax import lax
from jax.sharding import Mesh, PartitionSpec as P

WIDE = ("yh", "x", "c")
NARROW = ("z", "yl")
BF16 = jnp.bfloat16
F32 = jnp.float32


def gelu_parts(pre_values):
    values = pre_values.astype(F32)
    normal_cdf = 0.5 * (1.0 + jax.scipy.special.erf(values / math.sqrt(2.0)))
    normal_pdf = jnp.exp(-0.5 * values * values) / math.sqrt(2.0 * math.pi)
    return (values * normal_cdf, normal_cdf + values * normal_pdf)


def times_transposed(left, right):
    return lax.dot_general(
        left, right, (((1,), (1,)), ((), ())), preferred_element_type=F32
    )


def over_tokens(left, right):
    return lax.dot_general(
        left, right, (((0,), (0,)), ((), ())), preferred_element_type=F32
    )


def swap(values, axis):
    return lax.ppermute(values, axis, [(0, 1), (1, 0)])


def in_order(index, own, other):
    return (jnp.where(index == 0, own, other), jnp.where(index == 0, other, own))


def opposite(values):
    return lax.ppermute(values, ("c", "yl"), [(0, 3), (1, 2), (2, 1), (3, 0)])


def after(values, *results):
    return lax.optimization_barrier((values, *results))[0]


def whole(top, bottom):
    return lax.optimization_barrier(
        jnp.concatenate(
            [jnp.concatenate(top, axis=1), jnp.concatenate(bottom, axis=1)], axis=0
        )
    )


def per_device(layer_input, output_grad, pre_activation, w_up, w_down):
    core, lane = lax.axis_index("c"), lax.axis_index("yl")
    rows, width = layer_input.shape
    half = rows // 2
    hidden = pre_activation.shape[1]

    input_all = lax.all_gather(layer_input, WIDE, axis=0, tiled=True)

    down_lane = swap(w_down, "yl")
    down_core = swap(w_down, "c")
    pieces = jnp.broadcast_to(output_grad.reshape(2, half, width), (4, 2, half, width))
    grad_y = lax.all_to_all(pieces.reshape(8, half, width), ("yh", "yl"), 0, 0)
    grad_y = jnp.swapaxes(grad_y.reshape(4, 2, half, width), 1, 2)
    grad_y = grad_y.reshape(4, half, 2 * width)
    grad_y = after(grad_y, down_lane, down_core)
    grad_xy = lax.all_to_all(
        jnp.broadcast_to(grad_y, (4, 4, half, 2 * width)), "x", 0, 0
    )
    grad_xy = jnp.swapaxes(grad_xy, 0, 1)
    down_both = swap(down_lane, "c")
    down_cat = whole(
        in_order(lane, w_down, down_lane), in_order(lane, down_core, down_both)
    )
    grad_rows = grad_xy.reshape(-1, 2 * width)
    part = times_transposed(grad_rows, down_cat).astype(BF16)
    blocks = lax.all_to_all(part.reshape(8, rows, 2 * hidden), "z", 0, 0)

    up_after = after(w_up, part)
    up_lane = swap(up_after, "yl")
    up_core = swap(up_after, "c")
    up_both = opposite(up_after)
    up_cat = jnp.concatenate(
        [
            jnp.concatenate([w_up, up_core], axis=1),
            jnp.concatenate([up_lane, up_both], axis=1),
        ],
        axis=0,
    )

    pre_lane = swap(pre_activation, "yl")
    pre_both = jnp.stack(in_order(lane, pre_activation, after(pre_lane, grad_y)))
    pre_cut = pre_both.reshape(2, 2, 2, half, hidden)
    pre_half = jnp.where(lane == 0, pre_cut[:, :, 0], pre_cut[:, :, 1])
    pre_own, pre_sent = (
        jnp.where(core == 0, pre_half[:, i], pre_half[:, 1 - i]) for i in range(2)
    )
    pre_pair = swap(pre_sent, "c")
    pre_tile = jnp.concatenate([pre_own, pre_pair], axis=-1).reshape(rows, 2 * hidden)
    slope_factor = gelu_parts(pre_tile)[1]
    act_tile = gelu_parts(pre_both)[0].astype(BF16).reshape(-1, hidden)
    act_all = lax.all_gather(act_tile, "z", axis=0, tiled=True)

    act_grad = jnp.sum(blocks.astype(F32), axis=0)
    slope_tile = (act_grad * slope_factor).astype(BF16)
    slopes = lax.all_gather(slope_tile, "z", axis=0, tiled=True)

    part_in = times_transposed(slopes, up_cat).astype(BF16)
    part_in = jnp.swapaxes(part_in.reshape(4, 4, half, 2 * width), 0, 1)
    blocks = lax.all_to_all(part_in, "x", 0, 0)
    part_y = jnp.sum(blocks.astype(F32), axis=0).astype(BF16)
    part_y = jnp.stack(
        in_order(lane, part_y[..., :width], part_y[..., width:]), axis=1
    )
    blocks = lax.all_to_all(part_y.reshape(8, half, width), ("yh", "yl"), 0, 0)
    input_grad = jnp.sum(blocks.reshape(4, rows, width).astype(F32), axis=0).astype(BF16)

    grad_own, grad_pair = in_order(lane, grad_xy[..., :width], grad_xy[..., width:])
    grad_lane = swap(after(grad_pair, part), "yl")
    grad_core = jnp.stack(in_order(lane, grad_own, grad_lane), axis=2)
    grad_other = swap(after(grad_core, slopes), "c")
    grad_all = jnp.stack(in_order(core, grad_core, grad_other), axis=2)
    down_grad = over_tokens(act_all, grad_all.reshape(-1, width))

    slopes_core = swap(slopes[:, hidden:], "c")
    by_core = [
        jnp.stack(
            in_order(
                lane,
                kept.reshape(16, half, hidden),
                swap(kept, "yl").reshape(16, half, hidden),
            ),
            axis=1,
        )
        for kept in (slopes[:, :hidden], slopes_core)
    ]
    slopes_all = jnp.stack(in_order(core, by_core[0], by_core[1]), axis=1)
    up_grad = over_tokens(input_all, slopes_all.reshape(-1, hidden))
    return (input_grad, up_grad, down_grad)


def solution(mesh):
    fine = Mesh(mesh.devices.reshape(4, 4, 2, 8, 2), WIDE + NARROW)
    tokens = P(WIDE, NARROW)
    hidden = P(NARROW, WIDE)
    return jax.shard_map(
        per_device,
        mesh=fine,
        in_specs=(tokens, tokens, hidden, hidden, tokens),
        out_specs=(tokens, hidden, tokens),
        check_vma=False,
    )
```

```python
import math

import jax
import jax.numpy as jnp
from jax import lax
from jax.sharding import Mesh, PartitionSpec as P

WIDE = ("yh", "x", "c")
NARROW = ("z", "yl")
BF16 = jnp.bfloat16
F32 = jnp.float32


def gelu_parts(pre_values):
    values = pre_values.astype(F32)
    normal_cdf = 0.5 * (1.0 + jax.scipy.special.erf(values / math.sqrt(2.0)))
    normal_pdf = jnp.exp(-0.5 * values * values) / math.sqrt(2.0 * math.pi)
    return (values * normal_cdf, normal_cdf + values * normal_pdf)


def times_transposed(left, right):
    return lax.dot_general(
        left, right, (((1,), (1,)), ((), ())), preferred_element_type=F32
    )


def over_tokens(left, right):
    return lax.dot_general(
        left, right, (((0,), (0,)), ((), ())), preferred_element_type=F32
    )


def swap(values, axis):
    return lax.ppermute(values, axis, [(0, 1), (1, 0)])


def in_order(index, own, other):
    return (jnp.where(index == 0, own, other), jnp.where(index == 0, other, own))


def after(values, *results):
    return lax.optimization_barrier((values, *results))[0]


def tiled(top, bottom):
    return jnp.concatenate(
        [jnp.concatenate(top, axis=1), jnp.concatenate(bottom, axis=1)], axis=0
    )


def per_device(layer_input, output_grad, pre_activation, w_up, w_down):
    core, lane = lax.axis_index("c"), lax.axis_index("yl")
    rows, width = layer_input.shape
    half = rows // 2
    hidden = pre_activation.shape[1]

    input_all = lax.all_gather(layer_input, WIDE, axis=0, tiled=True)

    down_core = swap(w_down, "c")
    down_lane = swap(w_down, "yl")
    pieces = jnp.broadcast_to(output_grad.reshape(2, half, width), (4, 2, half, width))
    grad_y = lax.all_to_all(pieces.reshape(8, half, width), ("yh", "yl"), 0, 0)
    grad_y = grad_y.reshape(4, 2, half, width)
    grad_y = jnp.concatenate(in_order(lane, grad_y[:, 0], grad_y[:, 1]), axis=-1)
    grad_xy = lax.all_to_all(
        jnp.broadcast_to(grad_y, (4, 4, half, 2 * width)), "x", 0, 0
    )
    grad_xy = jnp.swapaxes(grad_xy, 0, 1)
    down_both = swap(down_lane, "c")
    grad_rows = grad_xy.reshape(-1, 2 * width)
    part = times_transposed(
        grad_rows[:, :width], jnp.concatenate([w_down, down_core], axis=0)
    )
    part = part + times_transposed(
        grad_rows[:, width:], jnp.concatenate([down_lane, down_both], axis=0)
    )
    part = part.astype(BF16)
    blocks = lax.all_to_all(part.reshape(8, rows, 2 * hidden), "z", 0, 0)

    up_after = after(w_up, part)
    up_lane = swap(up_after, "yl")
    up_core = swap(up_after, "c")
    up_both = swap(up_lane, "c")
    up_cat = tiled((w_up, up_core), (up_lane, up_both))

    pre_lane = swap(pre_activation, "yl")
    pre_both = jnp.stack(in_order(lane, pre_activation, after(pre_lane, grad_y)))
    pre_cut = pre_both.reshape(2, 2, 2, half, hidden)
    pre_half = jnp.where(lane == 0, pre_cut[:, :, 0], pre_cut[:, :, 1])
    pre_own, pre_sent = (
        jnp.where(core == 0, pre_half[:, i], pre_half[:, 1 - i]) for i in range(2)
    )
    pre_pair = swap(pre_sent, "c")
    pre_tile = jnp.concatenate([pre_own, pre_pair], axis=-1).reshape(rows, 2 * hidden)
    slope_factor = gelu_parts(pre_tile)[1]
    act_tile = gelu_parts(pre_both)[0].astype(BF16).reshape(-1, hidden)
    act_all = lax.all_gather(act_tile, "z", axis=0, tiled=True)

    act_grad = jnp.sum(blocks.astype(F32), axis=0)
    slope_tile = (act_grad * slope_factor).astype(BF16)
    slopes = lax.all_gather(slope_tile, "z", axis=0, tiled=True)

    part_in = times_transposed(slopes, up_cat).astype(BF16)
    part_in = jnp.swapaxes(part_in.reshape(4, 4, half, 2 * width), 0, 1)
    blocks = lax.all_to_all(part_in, "x", 0, 0)
    part_y = jnp.sum(blocks.astype(F32), axis=0).astype(BF16)
    part_y = jnp.stack(
        in_order(lane, part_y[..., :width], part_y[..., width:]), axis=1
    )
    blocks = lax.all_to_all(part_y.reshape(8, half, width), ("yh", "yl"), 0, 0)
    input_grad = jnp.sum(blocks.reshape(4, rows, width).astype(F32), axis=0).astype(BF16)

    grad_own, grad_pair = grad_xy[..., :width], grad_xy[..., width:]
    grad_lane = swap(after(grad_pair, part), "yl")
    grad_core = jnp.stack(in_order(lane, grad_own, grad_lane), axis=2)
    grad_other = swap(after(grad_core, slopes), "c")
    grad_all = jnp.stack(in_order(core, grad_core, grad_other), axis=2)
    down_grad = over_tokens(act_all, grad_all.reshape(-1, width))

    slopes_lane = swap(slopes, "yl")
    own = (slopes[:, :hidden], slopes_lane[:, :hidden])
    other = (
        swap(slopes[:, hidden:], "c"),
        swap(after(slopes_lane[:, hidden:], part_y), "c"),
    )
    by_core = [
        jnp.stack(in_order(lane, *(p.reshape(16, half, hidden) for p in pair)), axis=1)
        for pair in (own, other)
    ]
    slopes_all = jnp.stack(in_order(core, by_core[0], by_core[1]), axis=1)
    up_grad = over_tokens(input_all, slopes_all.reshape(-1, hidden))
    return (input_grad, up_grad, down_grad)


def solution(mesh):
    fine = Mesh(mesh.devices.reshape(4, 4, 2, 8, 2), WIDE + NARROW)
    tokens = P(WIDE, NARROW)
    hidden = P(NARROW, WIDE)
    return jax.shard_map(
        per_device,
        mesh=fine,
        in_specs=(tokens, tokens, hidden, hidden, tokens),
        out_specs=(tokens, hidden, tokens),
        check_vma=False,
    )
```

```python
import math

import jax
import jax.numpy as jnp
from jax import lax
from jax.sharding import Mesh, PartitionSpec as P

WIDE = ("yh", "x", "c")
NARROW = ("z", "yl")
BF16 = jnp.bfloat16
F32 = jnp.float32


def gelu_parts(pre_values):
    values = pre_values.astype(F32)
    normal_cdf = 0.5 * (1.0 + jax.scipy.special.erf(values / math.sqrt(2.0)))
    normal_pdf = jnp.exp(-0.5 * values * values) / math.sqrt(2.0 * math.pi)
    return (values * normal_cdf, normal_cdf + values * normal_pdf)


def times_transposed(left, right):
    return lax.dot_general(
        left, right, (((1,), (1,)), ((), ())), preferred_element_type=F32
    )


def over_tokens(left, right):
    return lax.dot_general(
        left, right, (((0,), (0,)), ((), ())), preferred_element_type=F32
    )


def swap(values, axis):
    return lax.ppermute(values, axis, [(0, 1), (1, 0)])


def in_order(index, own, other):
    return (jnp.where(index == 0, own, other), jnp.where(index == 0, other, own))


def opposite(values):
    return lax.ppermute(values, ("c", "yl"), [(0, 3), (1, 2), (2, 1), (3, 0)])


def after(values, *results):
    return lax.optimization_barrier((values, *results))[0]


def tiled(top, bottom):
    return jnp.concatenate(
        [jnp.concatenate(top, axis=1), jnp.concatenate(bottom, axis=1)], axis=0
    )


def per_device(layer_input, output_grad, pre_activation, w_up, w_down):
    core, lane = lax.axis_index("c"), lax.axis_index("yl")
    rows, width = layer_input.shape
    half = rows // 2
    hidden = pre_activation.shape[1]

    input_all = lax.all_gather(layer_input, WIDE, axis=0, tiled=True)

    down_core = swap(w_down, "c")
    down_lane = swap(w_down, "yl")
    pieces = jnp.broadcast_to(output_grad.reshape(2, half, width), (4, 2, half, width))
    grad_y = lax.all_to_all(pieces.reshape(8, half, width), ("yh", "yl"), 0, 0)
    grad_y = grad_y.reshape(4, 2, half, width)
    grad_y = jnp.concatenate(in_order(lane, grad_y[:, 0], grad_y[:, 1]), axis=-1)
    grad_xy = lax.all_to_all(
        jnp.broadcast_to(grad_y, (4, 4, half, 2 * width)), "x", 0, 0
    )
    grad_xy = jnp.swapaxes(grad_xy, 0, 1)
    down_both = swap(down_lane, "c")
    grad_rows = grad_xy.reshape(-1, 2 * width)
    part = times_transposed(
        grad_rows[:, :width], jnp.concatenate([w_down, down_core], axis=0)
    )
    part = part + times_transposed(
        grad_rows[:, width:], jnp.concatenate([down_lane, down_both], axis=0)
    )
    part = part.astype(BF16)
    blocks = lax.all_to_all(part.reshape(8, rows, 2 * hidden), "z", 0, 0)

    up_after = after(w_up, part)
    up_lane = swap(up_after, "yl")
    up_core = swap(up_after, "c")
    up_both = opposite(up_after)
    up_cat = tiled((w_up, up_core), (up_lane, up_both))

    pre_lane = swap(pre_activation, "yl")
    pre_both = jnp.stack(in_order(lane, pre_activation, after(pre_lane, grad_y)))
    pre_cut = pre_both.reshape(2, 2, 2, half, hidden)
    pre_half = jnp.where(lane == 0, pre_cut[:, :, 0], pre_cut[:, :, 1])
    pre_own, pre_sent = (
        jnp.where(core == 0, pre_half[:, i], pre_half[:, 1 - i]) for i in range(2)
    )
    pre_pair = swap(pre_sent, "c")
    pre_tile = jnp.concatenate([pre_own, pre_pair], axis=-1).reshape(rows, 2 * hidden)
    slope_factor = gelu_parts(pre_tile)[1]
    act_tile = gelu_parts(pre_both)[0].astype(BF16).reshape(-1, hidden)
    act_all = lax.all_gather(act_tile, "z", axis=0, tiled=True)

    act_grad = jnp.sum(blocks.astype(F32), axis=0)
    slope_tile = (act_grad * slope_factor).astype(BF16)
    slopes = lax.all_gather(slope_tile, "z", axis=0, tiled=True)

    part_in = times_transposed(slopes, up_cat).astype(BF16)
    part_in = jnp.swapaxes(part_in.reshape(4, 4, half, 2 * width), 0, 1)
    blocks = lax.all_to_all(part_in, "x", 0, 0)
    part_y = jnp.sum(blocks.astype(F32), axis=0).astype(BF16)
    part_y = jnp.stack(
        in_order(lane, part_y[..., :width], part_y[..., width:]), axis=1
    )
    blocks = lax.all_to_all(part_y.reshape(8, half, width), ("yh", "yl"), 0, 0)
    input_grad = jnp.sum(blocks.reshape(4, rows, width).astype(F32), axis=0).astype(BF16)

    grad_own, grad_pair = grad_xy[..., :width], grad_xy[..., width:]
    grad_lane = swap(after(grad_pair, part), "yl")
    grad_core = jnp.stack(in_order(lane, grad_own, grad_lane), axis=2)
    grad_other = swap(after(grad_core, slopes), "c")
    grad_all = jnp.stack(in_order(core, grad_core, grad_other), axis=2)
    down_grad = over_tokens(act_all, grad_all.reshape(-1, width))

    slopes_lane = swap(slopes, "yl")
    own = (slopes[:, :hidden], slopes_lane[:, :hidden])
    other = (
        swap(slopes[:, hidden:], "c"),
        swap(slopes_lane[:, hidden:], "c"),
    )
    by_core = [
        jnp.stack(in_order(lane, *(p.reshape(16, half, hidden) for p in pair)), axis=1)
        for pair in (own, other)
    ]
    slopes_all = jnp.stack(in_order(core, by_core[0], by_core[1]), axis=1)
    up_grad = over_tokens(after(input_all, slopes_lane), slopes_all.reshape(-1, hidden))
    return (input_grad, up_grad, down_grad)


def solution(mesh):
    fine = Mesh(mesh.devices.reshape(4, 4, 2, 8, 2), WIDE + NARROW)
    tokens = P(WIDE, NARROW)
    hidden = P(NARROW, WIDE)
    return jax.shard_map(
        per_device,
        mesh=fine,
        in_specs=(tokens, tokens, hidden, hidden, tokens),
        out_specs=(tokens, hidden, tokens),
        check_vma=False,
    )
```

```python
import math

import jax
import jax.numpy as jnp
from jax import lax
from jax.sharding import Mesh, PartitionSpec as P

WIDE = ("yh", "x", "c")
NARROW = ("z", "yl")
BF16 = jnp.bfloat16
F32 = jnp.float32


def gelu_parts(pre_values):
    values = pre_values.astype(F32)
    normal_cdf = 0.5 * (1.0 + jax.scipy.special.erf(values / math.sqrt(2.0)))
    normal_pdf = jnp.exp(-0.5 * values * values) / math.sqrt(2.0 * math.pi)
    return (values * normal_cdf, normal_cdf + values * normal_pdf)


def times_transposed(left, right):
    return lax.dot_general(
        left, right, (((1,), (1,)), ((), ())), preferred_element_type=F32
    )


def over_tokens(left, right):
    return lax.dot_general(
        left, right, (((0,), (0,)), ((), ())), preferred_element_type=F32
    )


def swap(values, axis):
    return lax.ppermute(values, axis, [(0, 1), (1, 0)])


def in_order(index, own, other):
    return (jnp.where(index == 0, own, other), jnp.where(index == 0, other, own))


def opposite(values):
    return lax.ppermute(values, ("c", "yl"), [(0, 3), (1, 2), (2, 1), (3, 0)])


def after(values, *results):
    return lax.optimization_barrier((values, *results))[0]


def tiled(top, bottom):
    return jnp.concatenate(
        [jnp.concatenate(top, axis=1), jnp.concatenate(bottom, axis=1)], axis=0
    )


def per_device(layer_input, output_grad, pre_activation, w_up, w_down):
    core, lane = lax.axis_index("c"), lax.axis_index("yl")
    rows, width = layer_input.shape
    half = rows // 2
    hidden = pre_activation.shape[1]

    input_all = lax.all_gather(layer_input, WIDE, axis=0, tiled=True)

    down_core = swap(w_down, "c")
    down_lane = swap(w_down, "yl")
    pieces = jnp.broadcast_to(output_grad.reshape(2, half, width), (4, 2, half, width))
    grad_y = lax.all_to_all(pieces.reshape(8, half, width), ("yh", "yl"), 0, 0)
    grad_y = grad_y.reshape(4, 2, half, width)
    grad_y = jnp.concatenate(in_order(lane, grad_y[:, 0], grad_y[:, 1]), axis=-1)
    grad_xy = lax.all_to_all(
        jnp.broadcast_to(grad_y, (4, 4, half, 2 * width)), "x", 0, 0
    )
    grad_xy = jnp.swapaxes(grad_xy, 0, 1)
    down_both = swap(down_lane, "c")
    grad_rows = grad_xy.reshape(-1, 2 * width)
    part = times_transposed(
        grad_rows[:, :width], jnp.concatenate([w_down, down_core], axis=0)
    )
    part = part + times_transposed(
        grad_rows[:, width:], jnp.concatenate([down_lane, down_both], axis=0)
    )
    part = part.astype(BF16)
    blocks = lax.all_to_all(part.reshape(8, rows, 2 * hidden), "z", 0, 0)

    up_after = after(w_up, part)
    up_lane = swap(up_after, "yl")
    up_core = swap(up_after, "c")
    up_both = opposite(up_after)
    up_cat = tiled((w_up, up_core), (up_lane, up_both))

    pre_lane = swap(pre_activation, "yl")
    pre_both = jnp.stack(in_order(lane, pre_activation, after(pre_lane, grad_y)))
    pre_cut = pre_both.reshape(2, 2, 2, half, hidden)
    pre_half = jnp.where(lane == 0, pre_cut[:, :, 0], pre_cut[:, :, 1])
    pre_own, pre_sent = (
        jnp.where(core == 0, pre_half[:, i], pre_half[:, 1 - i]) for i in range(2)
    )
    pre_pair = swap(pre_sent, "c")
    pre_tile = jnp.concatenate([pre_own, pre_pair], axis=-1).reshape(rows, 2 * hidden)
    slope_factor = gelu_parts(pre_tile)[1]
    act_tile = gelu_parts(pre_both)[0].astype(BF16).reshape(-1, hidden)
    act_all = lax.all_gather(act_tile, "z", axis=0, tiled=True)

    act_grad = jnp.sum(blocks.astype(F32), axis=0)
    slope_tile = (act_grad * slope_factor).astype(BF16)
    slopes = lax.all_gather(slope_tile, "z", axis=0, tiled=True)

    grad_own, grad_pair = grad_xy[..., :width], grad_xy[..., width:]
    grad_lane = swap(after(grad_pair, part), "yl")
    grad_core = jnp.stack(in_order(lane, grad_own, grad_lane), axis=2)
    grad_other = swap(grad_core, "c")
    grad_all = jnp.stack(in_order(core, grad_core, grad_other), axis=2)
    down_grad = over_tokens(act_all, after(grad_all, input_all).reshape(-1, width))

    part_in = times_transposed(slopes, up_cat).astype(BF16)
    part_in = jnp.swapaxes(part_in.reshape(4, 4, half, 2 * width), 0, 1)
    blocks = lax.all_to_all(part_in, "x", 0, 0)
    blocks = after(blocks, down_grad)
    part_y = jnp.sum(blocks.astype(F32), axis=0).astype(BF16)
    part_y = jnp.stack(
        in_order(lane, part_y[..., :width], part_y[..., width:]), axis=1
    )
    blocks = lax.all_to_all(part_y.reshape(8, half, width), ("yh", "yl"), 0, 0)
    input_grad = jnp.sum(blocks.reshape(4, rows, width).astype(F32), axis=0).astype(BF16)

    slopes_lane = swap(slopes, "yl")
    own = (slopes[:, :hidden], slopes_lane[:, :hidden])
    other = (
        swap(slopes[:, hidden:], "c"),
        swap(slopes_lane[:, hidden:], "c"),
    )
    by_core = [
        jnp.stack(in_order(lane, *(p.reshape(16, half, hidden) for p in pair)), axis=1)
        for pair in (own, other)
    ]
    slopes_all = jnp.stack(in_order(core, by_core[0], by_core[1]), axis=1)
    up_grad = over_tokens(after(input_all, slopes_lane), slopes_all.reshape(-1, hidden))
    return (input_grad, up_grad, down_grad)


def solution(mesh):
    fine = Mesh(mesh.devices.reshape(4, 4, 2, 8, 2), WIDE + NARROW)
    tokens = P(WIDE, NARROW)
    hidden = P(NARROW, WIDE)
    return jax.shard_map(
        per_device,
        mesh=fine,
        in_specs=(tokens, tokens, hidden, hidden, tokens),
        out_specs=(tokens, hidden, tokens),
        check_vma=False,
    )
```

```python
import math

import jax
import jax.numpy as jnp
from jax import lax
from jax.sharding import Mesh, PartitionSpec as P

WIDE = ("yh", "x", "c")
NARROW = ("z", "yl")
BF16 = jnp.bfloat16
F32 = jnp.float32


def gelu_parts(pre_values):
    values = pre_values.astype(F32)
    normal_cdf = 0.5 * (1.0 + jax.scipy.special.erf(values / math.sqrt(2.0)))
    normal_pdf = jnp.exp(-0.5 * values * values) / math.sqrt(2.0 * math.pi)
    return (values * normal_cdf, normal_cdf + values * normal_pdf)


def times_transposed(left, right):
    return lax.dot_general(
        left, right, (((1,), (1,)), ((), ())), preferred_element_type=F32
    )


def over_tokens(left, right):
    return lax.dot_general(
        left, right, (((0,), (0,)), ((), ())), preferred_element_type=F32
    )


def swap(values, axis):
    return lax.ppermute(values, axis, [(0, 1), (1, 0)])


def in_order(index, own, other):
    return (jnp.where(index == 0, own, other), jnp.where(index == 0, other, own))


def opposite(values):
    return lax.ppermute(values, ("c", "yl"), [(0, 3), (1, 2), (2, 1), (3, 0)])


def after(values, *results):
    return lax.optimization_barrier((values, *results))[0]


def tiled(top, bottom):
    return jnp.concatenate(
        [jnp.concatenate(top, axis=1), jnp.concatenate(bottom, axis=1)], axis=0
    )


def per_device(layer_input, output_grad, pre_activation, w_up, w_down):
    core, lane = lax.axis_index("c"), lax.axis_index("yl")
    rows, width = layer_input.shape
    half = rows // 2
    hidden = pre_activation.shape[1]

    input_all = lax.all_gather(layer_input, WIDE, axis=0, tiled=True)

    down_core = swap(w_down, "c")
    down_lane = swap(w_down, "yl")
    pieces = jnp.broadcast_to(output_grad.reshape(2, half, width), (4, 2, half, width))
    grad_y = lax.all_to_all(pieces.reshape(8, half, width), ("yh", "yl"), 0, 0)
    pre_lane = swap(pre_activation, "yl")
    grad_y = after(grad_y, pre_lane).reshape(4, 2, half, width)
    grad_y = jnp.concatenate(in_order(lane, grad_y[:, 0], grad_y[:, 1]), axis=-1)
    grad_xy = lax.all_to_all(
        jnp.broadcast_to(grad_y, (4, 4, half, 2 * width)), "x", 0, 0
    )
    grad_xy = jnp.swapaxes(grad_xy, 0, 1)
    down_both = swap(down_lane, "c")
    grad_rows = grad_xy.reshape(-1, 2 * width)
    part = times_transposed(
        grad_rows[:, :width], jnp.concatenate([w_down, down_core], axis=0)
    )
    part = part + times_transposed(
        grad_rows[:, width:], jnp.concatenate([down_lane, down_both], axis=0)
    )
    part = part.astype(BF16)
    blocks = lax.all_to_all(part.reshape(8, rows, 2 * hidden), "z", 0, 0)

    up_after = after(w_up, part)
    up_lane = swap(up_after, "yl")
    up_core = swap(up_after, "c")
    up_both = opposite(up_after)
    up_cat = tiled((w_up, up_core), (up_lane, up_both))

    pre_both = jnp.stack(in_order(lane, pre_activation, pre_lane))
    pre_cut = pre_both.reshape(2, 2, 2, half, hidden)
    pre_half = jnp.where(lane == 0, pre_cut[:, :, 0], pre_cut[:, :, 1])
    pre_own, pre_sent = (
        jnp.where(core == 0, pre_half[:, i], pre_half[:, 1 - i]) for i in range(2)
    )
    pre_pair = swap(pre_sent, "c")
    pre_tile = jnp.concatenate([pre_own, pre_pair], axis=-1).reshape(rows, 2 * hidden)
    slope_factor = gelu_parts(pre_tile)[1]
    act_tile = gelu_parts(pre_both)[0].astype(BF16).reshape(-1, hidden)
    act_all = lax.all_gather(act_tile, "z", axis=0, tiled=True)

    act_grad = jnp.sum(blocks.astype(F32), axis=0)
    slope_tile = (act_grad * slope_factor).astype(BF16)
    slopes = lax.all_gather(slope_tile, "z", axis=0, tiled=True)

    grad_own, grad_pair = grad_xy[..., :width], grad_xy[..., width:]
    grad_lane = swap(after(grad_pair, part), "yl")
    grad_core = jnp.stack(in_order(lane, grad_own, grad_lane), axis=2)
    grad_other = swap(grad_core, "c")
    grad_all = jnp.stack(in_order(core, grad_core, grad_other), axis=2)
    down_grad = over_tokens(act_all, after(grad_all, input_all).reshape(-1, width))

    part_in = times_transposed(slopes, up_cat).astype(BF16)
    part_in = jnp.swapaxes(part_in.reshape(4, 4, half, 2 * width), 0, 1)
    blocks = lax.all_to_all(part_in, "x", 0, 0)
    blocks = after(blocks, down_grad)
    part_y = jnp.sum(blocks.astype(F32), axis=0).astype(BF16)
    part_y = jnp.stack(
        in_order(lane, part_y[..., :width], part_y[..., width:]), axis=1
    )
    blocks = lax.all_to_all(part_y.reshape(8, half, width), ("yh", "yl"), 0, 0)
    input_grad = jnp.sum(blocks.reshape(4, rows, width).astype(F32), axis=0).astype(BF16)

    slopes_lane = swap(slopes, "yl")
    own = (slopes[:, :hidden], slopes_lane[:, :hidden])
    other = (
        swap(slopes[:, hidden:], "c"),
        swap(slopes_lane[:, hidden:], "c"),
    )
    by_core = [
        jnp.stack(in_order(lane, *(p.reshape(16, half, hidden) for p in pair)), axis=1)
        for pair in (own, other)
    ]
    slopes_all = jnp.stack(in_order(core, by_core[0], by_core[1]), axis=1)
    up_grad = over_tokens(after(input_all, slopes_lane), slopes_all.reshape(-1, hidden))
    return (input_grad, up_grad, down_grad)


def solution(mesh):
    fine = Mesh(mesh.devices.reshape(4, 4, 2, 8, 2), WIDE + NARROW)
    tokens = P(WIDE, NARROW)
    hidden = P(NARROW, WIDE)
    return jax.shard_map(
        per_device,
        mesh=fine,
        in_specs=(tokens, tokens, hidden, hidden, tokens),
        out_specs=(tokens, hidden, tokens),
        check_vma=False,
    )
```

```python
import math

import jax
import jax.numpy as jnp
from jax import lax
from jax.sharding import Mesh, PartitionSpec as P

WIDE = ("yh", "x", "c")
NARROW = ("z", "yl")
BF16 = jnp.bfloat16
F32 = jnp.float32


def gelu_parts(pre_values):
    values = pre_values.astype(F32)
    normal_cdf = 0.5 * (1.0 + jax.scipy.special.erf(values / math.sqrt(2.0)))
    normal_pdf = jnp.exp(-0.5 * values * values) / math.sqrt(2.0 * math.pi)
    return (values * normal_cdf, normal_cdf + values * normal_pdf)


def times_transposed(left, right):
    return lax.dot_general(
        left, right, (((1,), (1,)), ((), ())), preferred_element_type=F32
    )


def over_tokens(left, right):
    return lax.dot_general(
        left, right, (((0,), (0,)), ((), ())), preferred_element_type=F32
    )


def swap(values, axis):
    return lax.ppermute(values, axis, [(0, 1), (1, 0)])


def in_order(index, own, other):
    return (jnp.where(index == 0, own, other), jnp.where(index == 0, other, own))


def opposite(values):
    return lax.ppermute(values, ("c", "yl"), [(0, 3), (1, 2), (2, 1), (3, 0)])


def after(values, *results):
    return lax.optimization_barrier((values, *results))[0]


def tiled(top, bottom):
    return jnp.concatenate(
        [jnp.concatenate(top, axis=1), jnp.concatenate(bottom, axis=1)], axis=0
    )


def per_device(layer_input, output_grad, pre_activation, w_up, w_down):
    core, lane = lax.axis_index("c"), lax.axis_index("yl")
    rows, width = layer_input.shape
    half = rows // 2
    hidden = pre_activation.shape[1]

    input_all = lax.all_gather(layer_input, WIDE, axis=0, tiled=True)

    packed = jnp.concatenate([w_down, pre_activation], axis=0)
    pack_lane = swap(packed, "yl")
    down_lane, pre_lane = pack_lane[:hidden], pack_lane[hidden:]
    pieces = jnp.broadcast_to(output_grad.reshape(2, half, width), (4, 2, half, width))
    grad_y = lax.all_to_all(pieces.reshape(8, half, width), ("yh", "yl"), 0, 0)
    grad_y = grad_y.reshape(4, 2, half, width)
    grad_y = jnp.concatenate(in_order(lane, grad_y[:, 0], grad_y[:, 1]), axis=-1)
    grad_xy = lax.all_to_all(
        jnp.broadcast_to(grad_y, (4, 4, half, 2 * width)), "x", 0, 0
    )
    grad_xy = jnp.swapaxes(grad_xy, 0, 1)
    pack_core = swap(packed, "c")
    pack_both = swap(pack_lane, "c")
    down_core, pre_core = pack_core[:hidden], pack_core[hidden:]
    down_both, pre_diag = pack_both[:hidden], pack_both[hidden:]
    grad_rows = grad_xy.reshape(-1, 2 * width)
    part = times_transposed(
        grad_rows[:, :width], jnp.concatenate([w_down, down_core], axis=0)
    )
    part = part + times_transposed(
        grad_rows[:, width:], jnp.concatenate([down_lane, down_both], axis=0)
    )
    part = part.astype(BF16)
    blocks = lax.all_to_all(part.reshape(8, rows, 2 * hidden), "z", 0, 0)

    grad_own, grad_pair = grad_xy[..., :width], grad_xy[..., width:]
    grad_lane = swap(after(grad_pair, part), "yl")
    up_after = after(w_up, grad_lane)
    up_lane = swap(up_after, "yl")
    up_core = swap(up_after, "c")
    up_both = opposite(up_after)
    up_cat = tiled((w_up, up_core), (up_lane, up_both))

    def share(own, pair):
        cut = jnp.stack(in_order(lane, own, pair)).reshape(2, 2, 2, half, hidden)
        cut = jnp.where(lane == 0, cut[:, :, 0], cut[:, :, 1])
        return jnp.where(core == 0, cut[:, 0], cut[:, 1]).reshape(rows, hidden)

    pre_tile = jnp.concatenate(
        [share(pre_activation, pre_lane), share(pre_core, pre_diag)], axis=-1
    )
    pre_both = jnp.stack(in_order(lane, pre_activation, pre_lane))
    slope_factor = gelu_parts(pre_tile)[1]
    act_tile = gelu_parts(pre_both)[0].astype(BF16).reshape(-1, hidden)
    act_all = lax.all_gather(act_tile, "z", axis=0, tiled=True)

    act_grad = jnp.sum(blocks.astype(F32), axis=0)
    slope_tile = (act_grad * slope_factor).astype(BF16)
    slopes = lax.all_gather(slope_tile, "z", axis=0, tiled=True)

    grad_core = jnp.stack(in_order(lane, grad_own, grad_lane), axis=2)
    grad_other = swap(grad_core, "c")
    grad_all = jnp.stack(in_order(core, grad_core, grad_other), axis=2)
    down_grad = over_tokens(act_all, after(grad_all, input_all).reshape(-1, width))

    part_in = times_transposed(slopes, up_cat).astype(BF16)
    part_in = jnp.swapaxes(part_in.reshape(4, 4, half, 2 * width), 0, 1)
    blocks = lax.all_to_all(part_in, "x", 0, 0)
    blocks = after(blocks, down_grad)
    part_y = jnp.sum(blocks.astype(F32), axis=0).astype(BF16)
    part_y = jnp.stack(
        in_order(lane, part_y[..., :width], part_y[..., width:]), axis=1
    )
    blocks = lax.all_to_all(part_y.reshape(8, half, width), ("yh", "yl"), 0, 0)
    input_grad = jnp.sum(blocks.reshape(4, rows, width).astype(F32), axis=0).astype(BF16)

    slopes_lane = swap(slopes, "yl")
    own = (slopes[:, :hidden], slopes_lane[:, :hidden])
    other = (
        swap(slopes[:, hidden:], "c"),
        swap(slopes_lane[:, hidden:], "c"),
    )
    by_core = [
        jnp.stack(in_order(lane, *(p.reshape(16, half, hidden) for p in pair)), axis=1)
        for pair in (own, other)
    ]
    slopes_all = jnp.stack(in_order(core, by_core[0], by_core[1]), axis=1)
    up_grad = over_tokens(after(input_all, slopes_lane), slopes_all.reshape(-1, hidden))
    return (input_grad, up_grad, down_grad)


def solution(mesh):
    fine = Mesh(mesh.devices.reshape(4, 4, 2, 8, 2), WIDE + NARROW)
    tokens = P(WIDE, NARROW)
    hidden = P(NARROW, WIDE)
    return jax.shard_map(
        per_device,
        mesh=fine,
        in_specs=(tokens, tokens, hidden, hidden, tokens),
        out_specs=(tokens, hidden, tokens),
        check_vma=False,
    )
```

```python
import math

import jax
import jax.numpy as jnp
from jax import lax
from jax.sharding import Mesh, PartitionSpec as P

WIDE = ("yh", "x", "c")
NARROW = ("z", "yl")
BF16 = jnp.bfloat16
F32 = jnp.float32


def gelu_parts(pre_values):
    values = pre_values.astype(F32)
    normal_cdf = 0.5 * (1.0 + jax.scipy.special.erf(values / math.sqrt(2.0)))
    normal_pdf = jnp.exp(-0.5 * values * values) / math.sqrt(2.0 * math.pi)
    return (values * normal_cdf, normal_cdf + values * normal_pdf)


def times_transposed(left, right):
    return lax.dot_general(
        left, right, (((1,), (1,)), ((), ())), preferred_element_type=F32
    )


def over_tokens(left, right):
    return lax.dot_general(
        left, right, (((0,), (0,)), ((), ())), preferred_element_type=F32
    )


def swap(values, axis):
    return lax.ppermute(values, axis, [(0, 1), (1, 0)])


def in_order(index, own, other):
    return (jnp.where(index == 0, own, other), jnp.where(index == 0, other, own))


def opposite(values):
    return lax.ppermute(values, ("c", "yl"), [(0, 3), (1, 2), (2, 1), (3, 0)])


def after(values, *results):
    return lax.optimization_barrier((values, *results))[0]


def tiled(top, bottom):
    return jnp.concatenate(
        [jnp.concatenate(top, axis=1), jnp.concatenate(bottom, axis=1)], axis=0
    )


def per_device(layer_input, output_grad, pre_activation, w_up, w_down):
    core, lane = lax.axis_index("c"), lax.axis_index("yl")
    rows, width = layer_input.shape
    half = rows // 2
    hidden = pre_activation.shape[1]

    input_all = lax.all_gather(layer_input, WIDE, axis=0, tiled=True)

    down_core = swap(w_down, "c")
    down_lane = swap(w_down, "yl")
    pieces = jnp.broadcast_to(output_grad.reshape(2, half, width), (4, 2, half, width))
    grad_y = lax.all_to_all(pieces.reshape(8, half, width), ("yh", "yl"), 0, 0)
    pre_lane = swap(pre_activation, "yl")
    grad_y = after(grad_y, pre_lane).reshape(4, 2, half, width)
    grad_y = jnp.concatenate(in_order(lane, grad_y[:, 0], grad_y[:, 1]), axis=-1)
    grad_xy = lax.all_to_all(
        jnp.broadcast_to(grad_y, (4, 4, half, 2 * width)), "x", 0, 0
    )
    grad_xy = jnp.swapaxes(grad_xy, 0, 1)
    down_both = swap(down_lane, "c")
    grad_rows = grad_xy.reshape(-1, 2 * width)
    part = times_transposed(
        grad_rows[:, :width], jnp.concatenate([w_down, down_core], axis=0)
    )
    part = part + times_transposed(
        grad_rows[:, width:], jnp.concatenate([down_lane, down_both], axis=0)
    )
    part = part.astype(BF16)
    blocks = lax.all_to_all(part.reshape(8, rows, 2 * hidden), "z", 0, 0)

    up_after = after(w_up, part)
    up_lane = swap(up_after, "yl")
    up_core = swap(up_after, "c")
    up_both = opposite(up_after)
    up_cat = tiled((w_up, up_core), (up_lane, up_both))

    pre_both = jnp.stack(in_order(lane, pre_activation, pre_lane))
    pre_cut = pre_both.reshape(2, 2, 2, half, hidden)
    pre_half = jnp.where(lane == 0, pre_cut[:, :, 0], pre_cut[:, :, 1])
    pre_own, pre_sent = (
        jnp.where(core == 0, pre_half[:, i], pre_half[:, 1 - i]) for i in range(2)
    )
    pre_pair = swap(pre_sent, "c")
    pre_tile = jnp.concatenate([pre_own, pre_pair], axis=-1).reshape(rows, 2 * hidden)
    slope_factor = gelu_parts(pre_tile)[1]
    act_tile = gelu_parts(pre_both)[0].astype(BF16).reshape(-1, hidden)
    act_all = lax.all_gather(act_tile, "z", axis=0, tiled=True)

    act_grad = jnp.sum(blocks.astype(F32), axis=0)
    slope_tile = (act_grad * slope_factor).astype(BF16)
    slopes = lax.all_gather(slope_tile, "z", axis=0, tiled=True)

    grad_own, grad_pair = grad_xy[..., :width], grad_xy[..., width:]
    grad_lane = swap(after(grad_pair, part), "yl")
    grad_core = jnp.stack(in_order(lane, grad_own, grad_lane), axis=2)
    grad_other = swap(grad_core, "c")
    grad_all = jnp.stack(in_order(core, grad_core, grad_other), axis=2)
    down_grad = over_tokens(act_all, after(grad_all, input_all).reshape(-1, width))

    part_in = times_transposed(slopes, up_cat).astype(BF16)
    slopes_core = swap(after(slopes, part_in), "c")
    part_in = jnp.swapaxes(part_in.reshape(4, 4, half, 2 * width), 0, 1)
    blocks = lax.all_to_all(part_in, "x", 0, 0)
    blocks = after(blocks, down_grad)
    part_y = jnp.sum(blocks.astype(F32), axis=0).astype(BF16)
    part_y = jnp.stack(
        in_order(lane, part_y[..., :width], part_y[..., width:]), axis=1
    )
    slopes_lane = after(swap(slopes, "yl"), part_y)
    own = (slopes[:, :hidden], slopes_lane[:, :hidden])
    other = (
        slopes_core[:, hidden:],
        swap(slopes_lane[:, hidden:], "c"),
    )
    by_core = [
        jnp.stack(in_order(lane, *(p.reshape(16, half, hidden) for p in pair)), axis=1)
        for pair in (own, other)
    ]
    slopes_all = jnp.stack(in_order(core, by_core[0], by_core[1]), axis=1)
    up_grad = over_tokens(after(input_all, slopes_lane), slopes_all.reshape(-1, hidden))
    blocks = lax.all_to_all(part_y.reshape(8, half, width), ("yh", "yl"), 0, 0)
    input_grad = jnp.sum(after(blocks, up_grad).reshape(4, rows, width).astype(F32), axis=0).astype(BF16)
    return (input_grad, up_grad, down_grad)


def solution(mesh):
    fine = Mesh(mesh.devices.reshape(4, 4, 2, 8, 2), WIDE + NARROW)
    tokens = P(WIDE, NARROW)
    hidden = P(NARROW, WIDE)
    return jax.shard_map(
        per_device,
        mesh=fine,
        in_specs=(tokens, tokens, hidden, hidden, tokens),
        out_specs=(tokens, hidden, tokens),
        check_vma=False,
    )
```

```python
import math

import jax
import jax.numpy as jnp
from jax import lax
from jax.sharding import Mesh, PartitionSpec as P

WIDE = ("yh", "x", "c")
NARROW = ("z", "yl")
BF16 = jnp.bfloat16
F32 = jnp.float32


def gelu_parts(pre_values):
    values = pre_values.astype(F32)
    normal_cdf = 0.5 * (1.0 + jax.scipy.special.erf(values / math.sqrt(2.0)))
    normal_pdf = jnp.exp(-0.5 * values * values) / math.sqrt(2.0 * math.pi)
    return (values * normal_cdf, normal_cdf + values * normal_pdf)


def times_transposed(left, right):
    return lax.dot_general(
        left, right, (((1,), (1,)), ((), ())), preferred_element_type=F32
    )


def over_tokens(left, right):
    return lax.dot_general(
        left, right, (((0,), (0,)), ((), ())), preferred_element_type=F32
    )


def swap(values, axis):
    return lax.ppermute(values, axis, [(0, 1), (1, 0)])


def in_order(index, own, other):
    return (jnp.where(index == 0, own, other), jnp.where(index == 0, other, own))


def opposite(values):
    return lax.ppermute(values, ("c", "yl"), [(0, 3), (1, 2), (2, 1), (3, 0)])


def after(values, *results):
    return lax.optimization_barrier((values, *results))[0]


def tiled(top, bottom):
    return jnp.concatenate(
        [jnp.concatenate(top, axis=1), jnp.concatenate(bottom, axis=1)], axis=0
    )


def per_device(layer_input, output_grad, pre_activation, w_up, w_down):
    core, lane = lax.axis_index("c"), lax.axis_index("yl")
    rows, width = layer_input.shape
    half = rows // 2
    hidden = pre_activation.shape[1]

    input_all = lax.all_gather(layer_input, WIDE, axis=0, tiled=True)

    down_lane = swap(w_down, "yl")
    pieces = jnp.broadcast_to(output_grad.reshape(2, half, width), (4, 2, half, width))
    grad_y = lax.all_to_all(pieces.reshape(8, half, width), ("yh", "yl"), 0, 0)
    pre_lane = swap(pre_activation, "yl")
    grad_y = after(grad_y, pre_lane).reshape(4, 2, half, width)
    grad_y = jnp.concatenate(in_order(lane, grad_y[:, 0], grad_y[:, 1]), axis=-1)
    grad_xy = lax.all_to_all(
        jnp.broadcast_to(grad_y, (4, 4, half, 2 * width)), "x", 0, 0
    )
    grad_xy = jnp.swapaxes(grad_xy, 0, 1)
    down_core = swap(after(w_down, grad_y), "c")
    down_both = swap(down_lane, "c")
    grad_rows = grad_xy.reshape(-1, 2 * width)
    part = times_transposed(
        grad_rows[:, :width], jnp.concatenate([w_down, down_core], axis=0)
    )
    part = part + times_transposed(
        grad_rows[:, width:], jnp.concatenate([down_lane, down_both], axis=0)
    )
    part = part.astype(BF16)
    blocks = lax.all_to_all(part.reshape(8, rows, 2 * hidden), "z", 0, 0)

    up_after = after(w_up, part)
    up_lane = swap(up_after, "yl")
    up_core = swap(up_after, "c")
    up_both = opposite(up_after)
    up_cat = tiled((w_up, up_core), (up_lane, up_both))

    pre_both = jnp.stack(in_order(lane, pre_activation, pre_lane))
    pre_cut = pre_both.reshape(2, 2, 2, half, hidden)
    pre_half = jnp.where(lane == 0, pre_cut[:, :, 0], pre_cut[:, :, 1])
    pre_own, pre_sent = (
        jnp.where(core == 0, pre_half[:, i], pre_half[:, 1 - i]) for i in range(2)
    )
    pre_pair = swap(pre_sent, "c")
    pre_tile = jnp.concatenate([pre_own, pre_pair], axis=-1).reshape(rows, 2 * hidden)
    slope_factor = gelu_parts(pre_tile)[1]
    act_tile = gelu_parts(pre_both)[0].astype(BF16).reshape(-1, hidden)
    act_all = lax.all_gather(act_tile, "z", axis=0, tiled=True)

    act_grad = jnp.sum(blocks.astype(F32), axis=0)
    slope_tile = (act_grad * slope_factor).astype(BF16)
    slopes = lax.all_gather(slope_tile, "z", axis=0, tiled=True)

    grad_own, grad_pair = grad_xy[..., :width], grad_xy[..., width:]
    grad_lane = swap(after(grad_pair, part), "yl")
    grad_core = jnp.stack(in_order(lane, grad_own, grad_lane), axis=2)
    grad_other = swap(grad_core, "c")
    grad_all = jnp.stack(in_order(core, grad_core, grad_other), axis=2)
    down_grad = over_tokens(act_all, after(grad_all, input_all).reshape(-1, width))

    part_in = times_transposed(slopes, up_cat).astype(BF16)
    slopes_core = swap(after(slopes, part_in), "c")
    part_in = jnp.swapaxes(part_in.reshape(4, 4, half, 2 * width), 0, 1)
    blocks = lax.all_to_all(part_in, "x", 0, 0)
    blocks = after(blocks, down_grad)
    part_y = jnp.sum(blocks.astype(F32), axis=0).astype(BF16)
    part_y = jnp.stack(
        in_order(lane, part_y[..., :width], part_y[..., width:]), axis=1
    )
    blocks = lax.all_to_all(part_y.reshape(8, half, width), ("yh", "yl"), 0, 0)
    input_grad = jnp.sum(blocks.reshape(4, rows, width).astype(F32), axis=0).astype(BF16)

    slopes_lane = swap(slopes, "yl")
    own = (slopes[:, :hidden], slopes_lane[:, :hidden])
    other = (
        slopes_core[:, hidden:],
        swap(slopes_lane[:, hidden:], "c"),
    )
    by_core = [
        jnp.stack(in_order(lane, *(p.reshape(16, half, hidden) for p in pair)), axis=1)
        for pair in (own, other)
    ]
    slopes_all = jnp.stack(in_order(core, by_core[0], by_core[1]), axis=1)
    up_grad = over_tokens(after(input_all, slopes_lane), slopes_all.reshape(-1, hidden))
    return (input_grad, up_grad, down_grad)


def solution(mesh):
    fine = Mesh(mesh.devices.reshape(4, 4, 2, 8, 2), WIDE + NARROW)
    tokens = P(WIDE, NARROW)
    hidden = P(NARROW, WIDE)
    return jax.shard_map(
        per_device,
        mesh=fine,
        in_specs=(tokens, tokens, hidden, hidden, tokens),
        out_specs=(tokens, hidden, tokens),
        check_vma=False,
    )
```
